128 devices in a mesh: seq: 4 (over z), vocab: 32 (over y, x, core).
Axes of the slice: x: 4, y: 4, z: 4, core: 2. Of those that a mesh axis runs over, the one named last changes fastest.
Arguments:
- hidden: bfloat16 [2048, 5376], P('seq', 'vocab'), may hold values from -64 to 64
- embed_cotangent: bfloat16 [2048, 5376], P('seq', 'vocab'), may hold values from -24 to 24
- table: bfloat16 [24576, 5376], P('vocab'), may hold values from -3 to 3
- token_ids: int32 [2048], P('seq'), may hold values from 0 to 24575
- target_ids: int32 [2048], P('seq'), may hold values from 0 to 24575
- loss_scale: float32 [2048], P('seq'), may hold values from 8 to 32
Outputs:
- grad_hidden: bfloat16 [2048, 5376], P('seq', 'vocab')
- grad_table: float32 [24576, 5376], P('vocab', 'seq')
- token_loss: float32 [2048], P('seq')
The draws below stay inside these ranges and needn't reach their ends.
All inputs are finite; a program needn't handle non-finite values.
Results may differ from the reference program's by a relative error of at most 0.0047.
Values may be sent and summed in bfloat16 or wider, within the bound.
No kernel may reach another device: no remote copies, remote signals or barrier semaphores. Data moves between devices by JAX's collectives and lax.ppermute only.
A program may use at most 192 MiB of HBM per device.

```python
import math
import jax
import jax.numpy as jnp
import numpy as np
from jax import lax

D = 5376
VOCAB = 24576
TOKENS = 2048


def shared_table(key):
    spread = 3.3 / D ** 0.5
    entries = jax.random.normal(jax.random.fold_in(key, 7), (VOCAB, D), jnp.float32)
    return jnp.clip(entries, -6.0, 6.0) * spread


def draw_table(key, part):
    return shared_table(key).astype(jnp.bfloat16)


def draw_hidden(key, part):
    drawn_key = jax.random.fold_in(key, 11)
    entries = jnp.clip(jax.random.normal(drawn_key, (TOKENS, D), jnp.float32), -6.0, 6.0)
    return entries.astype(jnp.bfloat16)


def plant(values, own_key, least, largest):
    spot = [jax.random.randint(jax.random.fold_in(own_key, axis), (), 0, length) for axis, length in enumerate(values.shape)]
    longest = values.shape.index(max(values.shape))
    beside = spot[:longest] + [(spot[longest] + 1) % values.shape[longest]] + spot[longest + 1:]
    return values.at[tuple(spot)].set(least).at[tuple(beside)].set(largest)


def steps_of(rng, shape, shards, smallest, high):
    loudness, own = 1.0, jax.random.fold_in(rng, 6)
    for position, blocks in shards:
        steps = jnp.exp(jax.random.uniform(jax.random.fold_in(own, position), (blocks,), jnp.float32, smallest / len(shards), high / len(shards)))
        loudness = loudness * jnp.repeat(steps, shape[position] // blocks).reshape([-1 if axis == position else 1 for axis in range(len(shape))])
    return loudness


def cumulative_ranks(number_of, lean):
    portions = [(1 << 20) // math.isqrt(standing ** lean) + 1 for standing in range(1, number_of + 1)]
    scale = 1 + sum(portions) // (1 << 30)
    return np.cumsum(np.array([max(1, weight // scale) for weight in portions]))


def ranked(key, shape, amount, lean):
    listing = cumulative_ranks(amount, lean)
    ticket = jax.random.randint(jax.random.fold_in(key, 1), shape, 0, int(listing[amount - 1]))
    standing = jnp.searchsorted(jnp.asarray(listing, jnp.int32), ticket, side="right")
    return jax.random.permutation(jax.random.fold_in(key, 2), amount)[standing].astype(jnp.int32)


def normal_values(key, extent, scale, most, cuts=(), kind=jnp.bfloat16):
    values = jax.random.normal(key, extent, jnp.float32) * scale
    if len(cuts) > 0:
        values = steps_of(key, extent, cuts, -0.22, 0.18) * values
    return jnp.clip(values, min=-most, max=most).astype(kind)


def setup_inputs(seed: int = 0) -> dict:
    streams_of = jax.random.split(jax.random.key(seed), 7)
    return {
        "hidden": draw_hidden(jax.random.fold_in(streams_of[6], 71), 0),
        "embed_cotangent": normal_values(streams_of[1], (TOKENS, D), 4.0, 24.0, ((0, 4), (1, 32))),
        "table": draw_table(jax.random.fold_in(streams_of[6], 71), 0),
        "token_ids": plant(ranked(streams_of[3], (TOKENS,), VOCAB, 2), jax.random.fold_in(streams_of[3], 3), 0, VOCAB - 1).astype(jnp.int32),
        "target_ids": plant(jax.random.randint(streams_of[4], (TOKENS,), 0, VOCAB), jax.random.fold_in(streams_of[4], 1), 0, VOCAB - 1).astype(jnp.int32),
        "loss_scale": jnp.clip(jnp.exp(math.log(32.0) - 1.3862944 * jax.random.uniform(streams_of[5], (TOKENS,), jnp.float32) ** steps_of(streams_of[5], (TOKENS,), ((0, 4),), -0.2, 0.2)), 8.0, 32.0),
    }


def reference(hidden, embed_cotangent, table, token_ids, target_ids, loss_scale):
    logits = lax.dot_general(hidden, table, (((1,), (1,)), ((), ())), preferred_element_type=jnp.float32)
    vocab_ids = jnp.arange(table.shape[0], dtype=jnp.int32)
    target_hot = (target_ids[:, None] == vocab_ids[None, :]).astype(jnp.float32)
    row_top = jnp.max(logits, axis=1)
    exp_total = jnp.sum(jnp.exp(logits - row_top[:, None]), axis=1)
    target_logit = jnp.sum(logits * target_hot, axis=1)
    log_norm = row_top + jnp.log(exp_total)
    token_loss = log_norm - target_logit
    probability = jnp.exp(logits - log_norm[:, None])
    logit_grad = (loss_scale[:, None] * (probability - target_hot)).astype(jnp.bfloat16)
    grad_hidden = jnp.dot(logit_grad, table, preferred_element_type=jnp.float32).astype(jnp.bfloat16)
    head_part = lax.dot_general(logit_grad, hidden, (((0,), (0,)), ((), ())), preferred_element_type=jnp.float32)
    embed_part = jax.ops.segment_sum(embed_cotangent.astype(jnp.float32), token_ids, num_segments=table.shape[0])
    grad_table = head_part + embed_part
    return (grad_hidden, grad_table, token_loss)
```

```python
import jax
import jax.numpy as jnp
from jax import lax
from jax.sharding import PartitionSpec as P

BF, F32 = jnp.bfloat16, jnp.float32


def vocab_perm(move):
    pairs = []
    for v in range(32):
        y, x, c = move(v // 8, (v // 2) % 4, v % 2)
        pairs.append((v, (y % 4) * 8 + (x % 4) * 2 + c))
    return pairs


def send_x(a, d):
    return lax.ppermute(a, "vocab", vocab_perm(lambda y, x, c: (y, x + d, c)))


def send_y(a, d):
    return lax.ppermute(a, "vocab", vocab_perm(lambda y, x, c: (y + d, x, c)))


def send_core(a):
    return lax.ppermute(a, "vocab", vocab_perm(lambda y, x, c: (y, x, 1 - c)))


def send_z(a, d):
    return lax.ppermute(a, "seq", [(i, (i + d) % 4) for i in range(4)])


def swap_zy(a):
    pairs = []
    for z in range(4):
        for v in range(32):
            pairs.append((z * 32 + v, (v // 8) * 32 + z * 8 + v % 8))
    return lax.ppermute(a, ("seq", "vocab"), pairs)


def ring_gather(a, send, me, tie=None):
    low, high = send(a, 1), send(a, -1)
    half = a.shape[-1] // 2
    low_half, high_half = low[..., :half], high[..., half:]
    if tie is not None:
        low_half, high_half, tie = lax.optimization_barrier((low_half, high_half, tie))
    far_low, far_high = send(low_half, 1), send(high_half, -1)
    out = jnp.zeros((4,) + a.shape, a.dtype)
    out = lax.dynamic_update_index_in_dim(out, a, me, 0)
    out = lax.dynamic_update_index_in_dim(out, low, (me + 3) % 4, 0)
    out = lax.dynamic_update_index_in_dim(out, high, (me + 1) % 4, 0)
    far = jnp.concatenate([far_low, far_high], -1)
    out = lax.dynamic_update_index_in_dim(out, far, (me + 2) % 4, 0)
    return out if tie is None else (out,) + tuple(tie)


def both_cores(own, send, c):
    other = send(own)
    first, second = jnp.where(c == 0, own, other), jnp.where(c == 0, other, own)
    both = jnp.stack([first, second], 2).transpose(1, 2, 3, 0, 4)
    return both.reshape(both.shape[0] * both.shape[1] * both.shape[2], -1)


def scatter_send(q, send, me):
    pick = lambda d: lax.dynamic_index_in_dim(q, (me + d) % 4, 0, keepdims=False)
    return pick(0), [send(pick(d).astype(BF), d) for d in (1, 3, 2)]


def scatter_sum(own, got):
    return own + got[0].astype(F32) + got[1].astype(F32) + got[2].astype(F32)


def body(hidden, embed_cotangent, table, token_ids, target_ids, loss_scale):
    tie = lax.optimization_barrier
    z, v = lax.axis_index("seq"), lax.axis_index("vocab")
    y, x, c = v // 8, (v // 2) % 4, v % 2
    rows = table.shape[0]
    entry = v * rows + lax.broadcasted_iota(jnp.int32, (rows, 1), 0)
    hid, cot = hidden.T, embed_cotangent.T
    width, tokens = hid.shape

    high, low = token_ids // 256, token_ids % 256
    id_rows = jnp.stack([high, low]).astype(BF)
    cot = jnp.concatenate([cot, id_rows, jnp.zeros((6, tokens), BF)], 0)
    swapped = swap_zy(cot)
    across = ring_gather(hid, send_x, x)
    across, swapped = tie((across, swapped))

    table_t = table.T.reshape(16, 2, width, rows)
    own_part, table_t = ring_gather(across, send_y, y, (table_t,))
    own_table = lax.dynamic_index_in_dim(table_t, c, 1, keepdims=False).reshape(16 * width, rows)
    other_table = lax.dynamic_index_in_dim(table_t, 1 - c, 1, keepdims=False).reshape(16 * width, rows)
    own_part, own_table, other_table, swapped = tie((own_part, own_table, other_table, swapped))
    other_part = send_core(own_part)

    same_core = [[2 * k + i for k in range(16)] for i in range(2)]
    cot_own = lax.all_gather(swapped, "vocab", axis=0, axis_index_groups=same_core)

    pick_z = lambda d: lax.dynamic_index_in_dim(own_part, (z + d) % 4, 0, keepdims=False)
    hid_got = [send_z(pick_z(d), d) for d in (1, 3, 2)]

    first = (((0,), (0,)), ((), ()))
    last = (((1,), (1,)), ((), ()))
    plain = (((1,), (0,)), ((), ()))
    dot = lambda a, b, dims: lax.dot_general(a, b, dims, preferred_element_type=F32)
    logits = dot(own_table, own_part.reshape(16 * width, tokens), first)
    logits = logits + dot(other_table, other_part.reshape(16 * width, tokens), first)

    hot = target_ids[None, :] == entry
    top = jnp.max(logits, axis=0)
    total = jnp.sum(jnp.exp(logits - top[None, :]), axis=0)
    target = jnp.sum(jnp.where(hot, logits, 0.0), axis=0)
    stats = jnp.stack([top, total, target])
    stats = lax.all_to_all(jnp.broadcast_to(stats[None], (32,) + stats.shape), "vocab", 0, 0)
    row_top = jnp.max(stats[:, 0], axis=0)
    exp_total = jnp.sum(stats[:, 1] * jnp.exp(stats[:, 0] - row_top[None]), axis=0)
    target_logit = jnp.sum(stats[:, 2], axis=0)
    log_norm = row_top + jnp.log(exp_total)
    token_loss = log_norm - target_logit

    grad = loss_scale[None, :] * (jnp.exp(logits - log_norm[None, :]) - hot.astype(F32))
    grad = grad.astype(BF)
    grad_low, grad_high = send_z(grad, 1), send_z(grad, -1)

    away = dot(other_table, grad, plain).astype(BF)
    away, hid_got = tie((away, hid_got))
    back = send_core(away)
    mine = dot(own_table, grad, plain) + back.astype(F32)
    mine = mine.reshape(4, 4, width, tokens)
    half = tokens // 2
    a_own, a_got = scatter_send(mine[..., :half].transpose(1, 0, 2, 3), send_x, x)
    b_own, b_got = scatter_send(mine[..., half:], send_y, y)

    hid_all = both_cores(jnp.stack([pick_z(0)] + hid_got), send_core, c)
    cot_own = cot_own.reshape(4, 4, width + 8, tokens)
    ids = (cot_own[:, 0, width].astype(F32) * 256.0 + cot_own[:, 0, width + 1].astype(F32)).astype(jnp.int32)
    cot_all = both_cores(cot_own[:, :, :width], send_core, c)
    token_hot = (ids.reshape(1, 4 * tokens) == entry).astype(BF)
    embed_term = dot(cot_all, token_hot, last)

    a_got, b_got, grad_low, grad_high, embed_term = tie((a_got, b_got, grad_low, grad_high, embed_term))
    a_own, a_got = scatter_send(scatter_sum(a_own, a_got), send_y, y)
    b_own, b_got = scatter_send(scatter_sum(b_own, b_got), send_x, x)
    mid = rows // 2
    far_low, far_high = send_z(grad_low[:mid], 1), send_z(grad_high[mid:], -1)
    near = dot(hid_all[:, : 3 * tokens], jnp.concatenate([grad, grad_low, grad_high], 1), last)
    near = near + embed_term
    a_got, b_got, far_low, far_high, near = tie((a_got, b_got, far_low, far_high, near))
    grad_hidden = jnp.concatenate([scatter_sum(a_own, a_got), scatter_sum(b_own, b_got)], -1).astype(BF).T
    far = jnp.concatenate([far_low, far_high], 0)
    grad_table = near + dot(hid_all[:, 3 * tokens :], far, last)
    return (grad_hidden, grad_table.T, token_loss)


def solution(mesh):
    placed = (P("seq", "vocab"), P("seq", "vocab"), P("vocab", None), P("seq"), P("seq"), P("seq"))
    return jax.shard_map(
        body,
        mesh=mesh,
        in_specs=placed,
        out_specs=(P("seq", "vocab"), P("vocab", "seq"), P("seq")),
        check_vma=False,
    )
```

```python
import jax
import jax.numpy as jnp
from jax import lax
from jax.experimental import pallas as pl
from jax.experimental.pallas import tpu as pltpu
from jax.sharding import PartitionSpec as P

BF, F32 = jnp.bfloat16, jnp.float32


def vocab_perm(move):
    pairs = []
    for v in range(32):
        y, x, c = move(v // 8, (v // 2) % 4, v % 2)
        pairs.append((v, (y % 4) * 8 + (x % 4) * 2 + c))
    return pairs


def send_x(a, d):
    return lax.ppermute(a, "vocab", vocab_perm(lambda y, x, c: (y, x + d, c)))


def send_y(a, d):
    return lax.ppermute(a, "vocab", vocab_perm(lambda y, x, c: (y + d, x, c)))


def send_core(a):
    return lax.ppermute(a, "vocab", vocab_perm(lambda y, x, c: (y, x, 1 - c)))


def send_z(a, d):
    return lax.ppermute(a, "seq", [(i, (i + d) % 4) for i in range(4)])


def swap_zy(a):
    pairs = []
    for z in range(4):
        for v in range(32):
            pairs.append((z * 32 + v, (v // 8) * 32 + z * 8 + v % 8))
    return lax.ppermute(a, ("seq", "vocab"), pairs)


def ring_near(a, send):
    return send(a, 1), send(a, -1)


def ring_far(near, send):
    low, high = near
    half = low.shape[-1] // 2
    return send(low[..., :half], 1), send(high[..., half:], -1)


def ring_place(a, near, far, me):
    out = jnp.zeros((4,) + a.shape, a.dtype)
    out = lax.dynamic_update_index_in_dim(out, a, me, 0)
    out = lax.dynamic_update_index_in_dim(out, near[0], (me + 3) % 4, 0)
    out = lax.dynamic_update_index_in_dim(out, near[1], (me + 1) % 4, 0)
    return lax.dynamic_update_index_in_dim(out, jnp.concatenate(far, -1), (me + 2) % 4, 0)


PAD = 176
NN = (((1,), (0,)), ((), ()))


def mm(a, b):
    return lax.dot_general(a, b, NN, preferred_element_type=F32)


def hidden_kernel(own_ref, pair_ref, g_ref, pg_ref, out_ref, again_ref):
    again_ref[...] = g_ref[...]
    out_ref[...] = (mm(own_ref[...], g_ref[...]) + mm(pair_ref[...], pg_ref[...])).astype(BF)


def hidden_terms(own_table, pair_table, grad, pair_grad):
    rows, tokens = grad.shape
    columns, tile = own_table.shape[0], 672
    table = pl.BlockSpec((tile, rows), lambda i: (i, 0))
    whole = pl.BlockSpec((rows, tokens), lambda i: (0, 0))
    return pl.pallas_call(
        hidden_kernel,
        out_shape=[jax.ShapeDtypeStruct((columns, tokens), BF), jax.ShapeDtypeStruct((rows, tokens), BF)],
        grid=(columns // tile,),
        in_specs=[table, table, whole, whole],
        out_specs=[pl.BlockSpec((tile, tokens), lambda i: (i, 0)), whole],
        compiler_params=pltpu.CompilerParams(vmem_limit_bytes=56 << 20),
        cost_estimate=pl.CostEstimate(flops=4 << 30, bytes_accessed=12 << 20, transcendentals=0),
        name="hidden_terms",
    )(own_table, pair_table, grad, pair_grad)


NT = (((1,), (1,)), ((), ()))


def table_kernel(core_ref, *refs):
    cots, hids, grads = refs[:8], refs[8:16], refs[18:22]
    ids_ref, entry_ref, out_ref = refs[16], refs[17], refs[22]
    width, tile = out_ref.shape[2:]
    hots = [(ids_ref[k] == entry_ref[...]).astype(F32).astype(BF) for k in range(4)]
    for core in range(2):
        total = jnp.zeros((4 * width, tile), F32)
        for k in range(4):
            total += lax.dot_general(cots[2 * k + core][...], hots[k], NT, preferred_element_type=F32)
            total += lax.dot_general(hids[2 * k + core][...], grads[k][...], NT, preferred_element_type=F32)
        place = core_ref[0] if core == 0 else 1 - core_ref[0]
        out_ref[:, pl.ds(place, 1)] = total.reshape(4, 1, width, tile)


def table_terms(core, cots, hids, ids, entry, grads, width):
    rows, tokens = grads[0].shape
    tile = 256
    return pl.pallas_call(
        table_kernel,
        out_shape=jax.ShapeDtypeStruct((4, 2, width, rows), F32),
        grid_spec=pltpu.PrefetchScalarGridSpec(
            num_scalar_prefetch=1,
            grid=(rows // tile,),
            in_specs=[pl.BlockSpec((4 * width, tokens), lambda i, core: (0, 0))] * 16
            + [pl.BlockSpec((4, 1, tokens), lambda i, core: (0, 0, 0)), pl.BlockSpec((tile, 1), lambda i, core: (i, 0))]
            + [pl.BlockSpec((tile, tokens), lambda i, core: (i, 0))] * 4,
            out_specs=pl.BlockSpec((4, 2, width, tile), lambda i, core: (0, 0, 0, i)),
        ),
        compiler_params=pltpu.CompilerParams(vmem_limit_bytes=48 << 20),
        cost_estimate=pl.CostEstimate(flops=8 << 30, bytes_accessed=16 << 20, transcendentals=0),
        name="table_terms",
    )(core, *cots, *hids, ids, entry, *grads)


def body(hidden, embed_cotangent, table, token_ids, target_ids, loss_scale):
    tie = lax.optimization_barrier
    z, v = lax.axis_index("seq"), lax.axis_index("vocab")
    y, x, c = v // 8, (v // 2) % 4, v % 2
    rows = table.shape[0]
    entry = v * rows + lax.broadcasted_iota(jnp.int32, (rows, 1), 0)
    order = [z, (z + 3) % 4, (z + 1) % 4, (z + 2) % 4]
    hid, cot = hidden.T, embed_cotangent.T
    width, tokens = hid.shape
    same_core = [[2 * k + i for k in range(16)] for i in range(2)]
    first = (((0,), (0,)), ((), ()))
    dot = lambda a, b: lax.dot_general(a, b, first, preferred_element_type=F32)

    id_rows = jnp.stack([token_ids // 256, token_ids % 256]).astype(BF)
    gap = PAD - width
    both = jnp.concatenate([cot, id_rows, jnp.zeros((gap - 2, tokens), BF)], 0)
    both = swap_zy(both)
    hid_near = ring_near(hid, send_x)
    hid_far = ring_far(hid_near, send_x)
    across = ring_place(hid, hid_near, hid_far, x)
    across, both = tie((across, both))
    across_near = ring_near(across, send_y)
    table_t = table.T.reshape(16, 2, width, rows)
    across_near, table_t = tie((across_near, table_t))
    across_far = ring_far(across_near, send_y)
    own_table = lax.dynamic_index_in_dim(table_t, c, 1, keepdims=False).reshape(16 * width, rows)
    other_table = lax.dynamic_index_in_dim(table_t, 1 - c, 1, keepdims=False).reshape(16 * width, rows)
    own_part = ring_place(across, across_near, across_far, y)
    own_part, own_table, other_table, both = tie((own_part, own_table, other_table, both))
    cols = lax.all_gather(both, "vocab", axis=0, axis_index_groups=same_core)

    pick_z = lambda d, part=own_part: lax.dynamic_index_in_dim(part, (z + d) % 4, 0, keepdims=False).reshape(4 * width, tokens)
    opposite = pick_z(2)
    hid_low, hid_high = send_z(pick_z(1), 1), send_z(pick_z(3), -1)
    mid = tokens // 2
    pass_low, pass_high = send_z(opposite[:, :mid], 1), send_z(opposite[:, mid:], -1)
    own_part = own_part.reshape(16 * width, tokens)
    other_part = send_core(own_part)
    logits = dot(own_table, own_part)
    logits, other_part = tie((logits, other_part))
    logits = logits + dot(other_table, other_part)
    pair_table = send_core(other_table)
    hot = target_ids[None, :] == entry
    top = jnp.max(logits, axis=0)
    total = jnp.sum(jnp.exp(logits - top[None, :]), axis=0)
    target = jnp.sum(jnp.where(hot, logits, 0.0), axis=0)
    stats = jnp.stack([top, total, target])
    stats, hid_low, hid_high, pass_low, pass_high = tie((stats, hid_low, hid_high, pass_low, pass_high))
    hid_far = [send_z(pass_low, 1), send_z(pass_high, -1)]
    stats = lax.all_to_all(jnp.broadcast_to(stats[None], (32,) + stats.shape), "vocab", 0, 0)
    row_top = jnp.max(stats[:, 0], axis=0)
    exp_total = jnp.sum(stats[:, 1] * jnp.exp(stats[:, 0] - row_top[None]), axis=0)
    target_logit = jnp.sum(stats[:, 2], axis=0)
    log_norm = row_top + jnp.log(exp_total)
    token_loss = log_norm - target_logit

    grad = loss_scale[None, :] * (jnp.exp(logits - log_norm[None, :]) - hot.astype(F32))
    grad = grad.astype(BF)
    grads = [grad] + [send_z(grad, d) for d in (1, 3, 2)]
    pair_grad = send_core(grad)
    terms, again = hidden_terms(own_table, pair_table, grad, pair_grad)
    terms = lax.all_to_all(terms.reshape(16, width, tokens), "vocab", 0, 0, axis_index_groups=same_core)
    grads[0] = again
    cols, grads, hid_far = tie((cols, grads, hid_far))
    hid_got = [pick_z(0), hid_low, hid_high, jnp.concatenate(hid_far, 1)]
    cols = cols.reshape(4, 4, PAD, tokens)
    cots, hids, ids = [], [], []
    for block, hid_piece in zip(order, hid_got):
        piece = lax.dynamic_index_in_dim(cols, block, 0, keepdims=False)
        pair = piece[0, width : width + 2].astype(F32)
        ids.append((pair[0] * 256.0 + pair[1]).astype(jnp.int32))
        piece = piece[:, :width].reshape(4 * width, tokens)
        cots += [piece, send_core(piece)]
        hids += [hid_piece, send_core(hid_piece)]
    grad_table = table_terms(c.astype(jnp.int32)[None], cots, hids, jnp.stack(ids)[:, None], entry, grads, width)
    terms, grad_table = tie((terms, grad_table))
    grad_hidden = jnp.sum(terms.astype(F32), axis=0).astype(BF).T
    return (grad_hidden, grad_table.reshape(8 * width, rows).T, token_loss)


def solution(mesh):
    placed = (P("seq", "vocab"), P("seq", "vocab"), P("vocab", None), P("seq"), P("seq"), P("seq"))
    return jax.shard_map(
        body,
        mesh=mesh,
        in_specs=placed,
        out_specs=(P("seq", "vocab"), P("vocab", "seq"), P("seq")),
        check_vma=False,
    )
```

```python
import jax
import jax.numpy as jnp
from jax import lax
from jax.experimental import pallas as pl
from jax.experimental.pallas import tpu as pltpu
from jax.sharding import PartitionSpec as P

BF, F32 = jnp.bfloat16, jnp.float32


def vocab_perm(move):
    pairs = []
    for v in range(32):
        y, x, c = move(v // 8, (v // 2) % 4, v % 2)
        pairs.append((v, (y % 4) * 8 + (x % 4) * 2 + c))
    return pairs


def send_x(a, d):
    return lax.ppermute(a, "vocab", vocab_perm(lambda y, x, c: (y, x + d, c)))


def send_y(a, d):
    return lax.ppermute(a, "vocab", vocab_perm(lambda y, x, c: (y + d, x, c)))


def send_core(a):
    return lax.ppermute(a, "vocab", vocab_perm(lambda y, x, c: (y, x, 1 - c)))


def send_z(a, d):
    return lax.ppermute(a, "seq", [(i, (i + d) % 4) for i in range(4)])


def swap_zy(a):
    pairs = []
    for z in range(4):
        for v in range(32):
            pairs.append((z * 32 + v, (v // 8) * 32 + z * 8 + v % 8))
    return lax.ppermute(a, ("seq", "vocab"), pairs)


def ring_near(a, send):
    return send(a, 1), send(a, -1)


def ring_far(near, send):
    low, high = near
    half = low.shape[-1] // 2
    return send(low[..., :half], 1), send(high[..., half:], -1)


def ring_place(a, near, far, me):
    out = jnp.zeros((4,) + a.shape, a.dtype)
    out = lax.dynamic_update_index_in_dim(out, a, me, 0)
    out = lax.dynamic_update_index_in_dim(out, near[0], (me + 3) % 4, 0)
    out = lax.dynamic_update_index_in_dim(out, near[1], (me + 1) % 4, 0)
    return lax.dynamic_update_index_in_dim(out, jnp.concatenate(far, -1), (me + 2) % 4, 0)


PAD = 176
NN = (((1,), (0,)), ((), ()))


def mm(a, b):
    return lax.dot_general(a, b, NN, preferred_element_type=F32)


def hidden_kernel(own_ref, pair_ref, g_ref, pg_ref, out_ref, again_ref):
    again_ref[...] = g_ref[...]
    out_ref[...] = (mm(own_ref[...], g_ref[...]) + mm(pair_ref[...], pg_ref[...])).astype(BF)


def hidden_terms(own_table, pair_table, grad, pair_grad):
    rows, tokens = grad.shape
    columns, tile = own_table.shape[0], 672
    table = pl.BlockSpec((tile, rows), lambda i: (i, 0))
    whole = pl.BlockSpec((rows, tokens), lambda i: (0, 0))
    return pl.pallas_call(
        hidden_kernel,
        out_shape=[jax.ShapeDtypeStruct((columns, tokens), BF), jax.ShapeDtypeStruct((rows, tokens), BF)],
        grid=(columns // tile,),
        in_specs=[table, table, whole, whole],
        out_specs=[pl.BlockSpec((tile, tokens), lambda i: (i, 0)), whole],
        compiler_params=pltpu.CompilerParams(vmem_limit_bytes=56 << 20),
        cost_estimate=pl.CostEstimate(flops=4 << 30, bytes_accessed=12 << 20, transcendentals=0),
        name="hidden_terms",
    )(own_table, pair_table, grad, pair_grad)


NT = (((1,), (1,)), ((), ()))


def table_kernel(core_ref, *refs):
    cots, hids, grads = refs[:8], refs[8:16], refs[18:22]
    ids_ref, entry_ref, out_ref = refs[16], refs[17], refs[22]
    width, tile = out_ref.shape[2:]
    hots = [(ids_ref[k] == entry_ref[...]).astype(F32).astype(BF) for k in range(4)]
    for core in range(2):
        total = jnp.zeros((4 * width, tile), F32)
        for k in range(4):
            total += lax.dot_general(cots[2 * k + core][...], hots[k], NT, preferred_element_type=F32)
            total += lax.dot_general(hids[2 * k + core][...], grads[k][...], NT, preferred_element_type=F32)
        place = core_ref[0] if core == 0 else 1 - core_ref[0]
        out_ref[:, pl.ds(place, 1)] = total.reshape(4, 1, width, tile)


def table_terms(core, cots, hids, ids, entry, grads, width):
    rows, tokens = grads[0].shape
    tile = 256
    return pl.pallas_call(
        table_kernel,
        out_shape=jax.ShapeDtypeStruct((4, 2, width, rows), F32),
        grid_spec=pltpu.PrefetchScalarGridSpec(
            num_scalar_prefetch=1,
            grid=(rows // tile,),
            in_specs=[pl.BlockSpec((4 * width, tokens), lambda i, core: (0, 0))] * 16
            + [pl.BlockSpec((4, 1, tokens), lambda i, core: (0, 0, 0)), pl.BlockSpec((tile, 1), lambda i, core: (i, 0))]
            + [pl.BlockSpec((tile, tokens), lambda i, core: (i, 0))] * 4,
            out_specs=pl.BlockSpec((4, 2, width, tile), lambda i, core: (0, 0, 0, i)),
        ),
        compiler_params=pltpu.CompilerParams(vmem_limit_bytes=48 << 20),
        cost_estimate=pl.CostEstimate(flops=8 << 30, bytes_accessed=16 << 20, transcendentals=0),
        name="table_terms",
    )(core, *cots, *hids, ids, entry, *grads)


def body(hidden, embed_cotangent, table, token_ids, target_ids, loss_scale):
    tie = lax.optimization_barrier
    z, v = lax.axis_index("seq"), lax.axis_index("vocab")
    y, x, c = v // 8, (v // 2) % 4, v % 2
    rows = table.shape[0]
    entry = v * rows + lax.broadcasted_iota(jnp.int32, (rows, 1), 0)
    order = [z, (z + 3) % 4, (z + 1) % 4, (z + 2) % 4]
    hid, cot = hidden.T, embed_cotangent.T
    width, tokens = hid.shape
    same_core = [[2 * k + i for k in range(16)] for i in range(2)]
    first = (((0,), (0,)), ((), ()))
    dot = lambda a, b: lax.dot_general(a, b, first, preferred_element_type=F32)

    id_rows = jnp.stack([token_ids // 256, token_ids % 256]).astype(BF)
    gap = PAD - width
    both = jnp.concatenate([cot, id_rows, jnp.zeros((gap - 2, tokens), BF)], 0)
    both = swap_zy(both)
    hid_near = ring_near(hid, send_x)
    hid_far = ring_far(hid_near, send_x)
    across = ring_place(hid, hid_near, hid_far, x)
    across, both = tie((across, both))
    across_near = ring_near(across, send_y)
    table_t = table.T.reshape(16, 2, width, rows)
    across_near, table_t = tie((across_near, table_t))
    across_far = ring_far(across_near, send_y)
    own_table = lax.dynamic_index_in_dim(table_t, c, 1, keepdims=False).reshape(16 * width, rows)
    other_table = lax.dynamic_index_in_dim(table_t, 1 - c, 1, keepdims=False).reshape(16 * width, rows)
    own_part = ring_place(across, across_near, across_far, y)
    own_part, own_table, other_table, both = tie((own_part, own_table, other_table, both))
    cols = lax.all_gather(both, "vocab", axis=0, axis_index_groups=same_core)

    pick_z = lambda d, part=own_part: lax.dynamic_index_in_dim(part, (z + d) % 4, 0, keepdims=False).reshape(4 * width, tokens)
    opposite = pick_z(2)
    hid_low, hid_high = send_z(pick_z(1), 1), send_z(pick_z(3), -1)
    mid = tokens // 2
    pass_low, pass_high = send_z(opposite[:, :mid], 1), send_z(opposite[:, mid:], -1)
    own_part = own_part.reshape(16 * width, tokens)
    other_part = send_core(own_part)
    logits = dot(own_table, own_part)
    logits, other_part = tie((logits, other_part))
    logits = logits + dot(other_table, other_part)
    pair_table = send_core(other_table)
    hot = target_ids[None, :] == entry
    top = jnp.max(logits, axis=0)
    total = jnp.sum(jnp.exp(logits - top[None, :]), axis=0)
    target = jnp.sum(jnp.where(hot, logits, 0.0), axis=0)
    stats = jnp.stack([top, total, target])
    stats, hid_low, hid_high = tie((stats, hid_low, hid_high))
    stats = lax.all_to_all(jnp.broadcast_to(stats[None], (32,) + stats.shape), "vocab", 0, 0)
    stats, pass_low, pass_high = tie((stats, pass_low, pass_high))
    hid_far = [send_z(pass_low, 1), send_z(pass_high, -1)]
    row_top = jnp.max(stats[:, 0], axis=0)
    exp_total = jnp.sum(stats[:, 1] * jnp.exp(stats[:, 0] - row_top[None]), axis=0)
    target_logit = jnp.sum(stats[:, 2], axis=0)
    log_norm = row_top + jnp.log(exp_total)
    token_loss = log_norm - target_logit

    grad = loss_scale[None, :] * (jnp.exp(logits - log_norm[None, :]) - hot.astype(F32))
    grad = grad.astype(BF)
    grads = [grad] + [send_z(grad, d) for d in (1, 3, 2)]
    pair_grad = send_core(grad)
    terms, again = hidden_terms(own_table, pair_table, grad, pair_grad)
    terms = lax.all_to_all(terms.reshape(16, width, tokens), "vocab", 0, 0, axis_index_groups=same_core)
    grads[0] = again
    cols, grads, hid_far = tie((cols, grads, hid_far))
    hid_got = [pick_z(0), hid_low, hid_high, jnp.concatenate(hid_far, 1)]
    cols = cols.reshape(4, 4, PAD, tokens)
    cots, hids, ids = [], [], []
    for block, hid_piece in zip(order, hid_got):
        piece = lax.dynamic_index_in_dim(cols, block, 0, keepdims=False)
        pair = piece[0, width : width + 2].astype(F32)
        ids.append((pair[0] * 256.0 + pair[1]).astype(jnp.int32))
        piece = piece[:, :width].reshape(4 * width, tokens)
        cots += [piece, send_core(piece)]
        hids += [hid_piece, send_core(hid_piece)]
    grad_table = table_terms(c.astype(jnp.int32)[None], cots, hids, jnp.stack(ids)[:, None], entry, grads, width)
    terms, grad_table = tie((terms, grad_table))
    grad_hidden = jnp.sum(terms.astype(F32), axis=0).astype(BF).T
    return (grad_hidden, grad_table.reshape(8 * width, rows).T, token_loss)


def solution(mesh):
    placed = (P("seq", "vocab"), P("seq", "vocab"), P("vocab", None), P("seq"), P("seq"), P("seq"))
    return jax.shard_map(
        body,
        mesh=mesh,
        in_specs=placed,
        out_specs=(P("seq", "vocab"), P("vocab", "seq"), P("seq")),
        check_vma=False,
    )
```

```python
import jax
import jax.numpy as jnp
from jax import lax
from jax.experimental import pallas as pl
from jax.experimental.pallas import tpu as pltpu
from jax.sharding import PartitionSpec as P

BF, F32 = jnp.bfloat16, jnp.float32


def vocab_perm(move):
    pairs = []
    for v in range(32):
        y, x, c = move(v // 8, (v // 2) % 4, v % 2)
        pairs.append((v, (y % 4) * 8 + (x % 4) * 2 + c))
    return pairs


def send_x(a, d):
    return lax.ppermute(a, "vocab", vocab_perm(lambda y, x, c: (y, x + d, c)))


def send_y(a, d):
    return lax.ppermute(a, "vocab", vocab_perm(lambda y, x, c: (y + d, x, c)))


def send_core(a):
    return lax.ppermute(a, "vocab", vocab_perm(lambda y, x, c: (y, x, 1 - c)))


def send_z(a, d):
    return lax.ppermute(a, "seq", [(i, (i + d) % 4) for i in range(4)])


def swap_zy(a):
    pairs = []
    for z in range(4):
        for v in range(32):
            pairs.append((z * 32 + v, (v // 8) * 32 + z * 8 + v % 8))
    return lax.ppermute(a, ("seq", "vocab"), pairs)


def ring_near(a, send):
    return send(a, 1), send(a, -1)


def ring_far(near, send):
    low, high = near
    half = low.shape[-1] // 2
    return send(low[..., :half], 1), send(high[..., half:], -1)


def ring_place(a, near, far, me):
    out = jnp.zeros((4,) + a.shape, a.dtype)
    out = lax.dynamic_update_index_in_dim(out, a, me, 0)
    out = lax.dynamic_update_index_in_dim(out, near[0], (me + 3) % 4, 0)
    out = lax.dynamic_update_index_in_dim(out, near[1], (me + 1) % 4, 0)
    return lax.dynamic_update_index_in_dim(out, jnp.concatenate(far, -1), (me + 2) % 4, 0)


PAD = 176
NN = (((1,), (0,)), ((), ()))


def mm(a, b):
    return lax.dot_general(a, b, NN, preferred_element_type=F32)


def hidden_kernel(own_ref, pair_ref, g_ref, pg_ref, out_ref, again_ref):
    again_ref[...] = g_ref[...]
    out_ref[...] = (mm(own_ref[...], g_ref[...]) + mm(pair_ref[...], pg_ref[...])).astype(BF)


def hidden_terms(own_table, pair_table, grad, pair_grad):
    rows, tokens = grad.shape
    columns, tile = own_table.shape[0], 672
    table = pl.BlockSpec((tile, rows), lambda i: (i, 0))
    whole = pl.BlockSpec((rows, tokens), lambda i: (0, 0))
    return pl.pallas_call(
        hidden_kernel,
        out_shape=[jax.ShapeDtypeStruct((columns, tokens), BF), jax.ShapeDtypeStruct((rows, tokens), BF)],
        grid=(columns // tile,),
        in_specs=[table, table, whole, whole],
        out_specs=[pl.BlockSpec((tile, tokens), lambda i: (i, 0)), whole],
        compiler_params=pltpu.CompilerParams(vmem_limit_bytes=56 << 20),
        cost_estimate=pl.CostEstimate(flops=4 << 30, bytes_accessed=12 << 20, transcendentals=0),
        name="hidden_terms",
    )(own_table, pair_table, grad, pair_grad)


NT = (((1,), (1,)), ((), ()))


def near_kernel(*refs):
    cots, hids, grads = refs[:8], refs[8:14], refs[16:19]
    ids_ref, entry_ref, acc_ref = refs[14], refs[15], refs[19]
    hots = [(ids_ref[k] == entry_ref[...]).astype(F32).astype(BF) for k in range(4)]
    for core in range(2):
        total = lax.dot_general(cots[core][...], hots[0], NT, preferred_element_type=F32)
        for k in range(1, 4):
            total += lax.dot_general(cots[2 * k + core][...], hots[k], NT, preferred_element_type=F32)
        for k in range(3):
            total += lax.dot_general(hids[2 * k + core][...], grads[k][...], NT, preferred_element_type=F32)
        acc_ref[core] = total


def near_terms(cots, hids, ids, entry, grads):
    rows, tokens = grads[0].shape
    columns, tile = cots[0].shape[0], 256
    return pl.pallas_call(
        near_kernel,
        out_shape=jax.ShapeDtypeStruct((2, columns, rows), F32),
        grid=(rows // tile,),
        in_specs=[pl.BlockSpec((columns, tokens), lambda i: (0, 0))] * 14
        + [pl.BlockSpec((4, 1, tokens), lambda i: (0, 0, 0)), pl.BlockSpec((tile, 1), lambda i: (i, 0))]
        + [pl.BlockSpec((tile, tokens), lambda i: (i, 0))] * 3,
        out_specs=pl.BlockSpec((2, columns, tile), lambda i: (0, 0, i)),
        compiler_params=pltpu.CompilerParams(vmem_limit_bytes=48 << 20),
        cost_estimate=pl.CostEstimate(flops=1 << 30, bytes_accessed=1 << 20, transcendentals=0),
        name="near_terms",
    )(*cots, *hids, ids, entry, *grads)


def far_kernel(core_ref, acc_ref, own_ref, other_ref, g_ref, out_ref):
    width, tile = out_ref.shape[2:]
    for core, ref in enumerate((own_ref, other_ref)):
        total = acc_ref[core] + lax.dot_general(ref[...], g_ref[...], NT, preferred_element_type=F32)
        place = core_ref[0] if core == 0 else 1 - core_ref[0]
        out_ref[:, pl.ds(place, 1)] = total.reshape(4, 1, width, tile)


def far_terms(core, acc, own, other, grad, width):
    rows, tokens = grad.shape
    columns, tile = own.shape[0], 256
    piece = pl.BlockSpec((columns, tokens), lambda i, core: (0, 0))
    return pl.pallas_call(
        far_kernel,
        out_shape=jax.ShapeDtypeStruct((4, 2, width, rows), F32),
        grid_spec=pltpu.PrefetchScalarGridSpec(
            num_scalar_prefetch=1,
            grid=(rows // tile,),
            in_specs=[
                pl.BlockSpec((2, columns, tile), lambda i, core: (0, 0, i)),
                piece,
                piece,
                pl.BlockSpec((tile, tokens), lambda i, core: (i, 0)),
            ],
            out_specs=pl.BlockSpec((4, 2, width, tile), lambda i, core: (0, 0, 0, i)),
        ),
        compiler_params=pltpu.CompilerParams(vmem_limit_bytes=32 << 20),
        cost_estimate=pl.CostEstimate(flops=1 << 30, bytes_accessed=8 << 20, transcendentals=0),
        name="far_terms",
    )(core, acc, own, other, grad)


def body(hidden, embed_cotangent, table, token_ids, target_ids, loss_scale):
    tie = lax.optimization_barrier
    z, v = lax.axis_index("seq"), lax.axis_index("vocab")
    y, x, c = v // 8, (v // 2) % 4, v % 2
    rows = table.shape[0]
    entry = v * rows + lax.broadcasted_iota(jnp.int32, (rows, 1), 0)
    order = [z, (z + 3) % 4, (z + 1) % 4, (z + 2) % 4]
    hid, cot = hidden.T, embed_cotangent.T
    width, tokens = hid.shape
    same_core = [[2 * k + i for k in range(16)] for i in range(2)]
    first = (((0,), (0,)), ((), ()))
    dot = lambda a, b: lax.dot_general(a, b, first, preferred_element_type=F32)

    id_rows = jnp.stack([token_ids // 256, token_ids % 256]).astype(BF)
    gap = PAD - width
    both = jnp.concatenate([cot, id_rows, jnp.zeros((gap - 2, tokens), BF)], 0)
    both = swap_zy(both)
    hid_near = ring_near(hid, send_x)
    hid_far = ring_far(hid_near, send_x)
    across = ring_place(hid, hid_near, hid_far, x)
    across, both = tie((across, both))
    across_near = ring_near(across, send_y)
    table_t = table.T.reshape(16, 2, width, rows)
    across_near, table_t = tie((across_near, table_t))
    across_far = ring_far(across_near, send_y)
    own_table = lax.dynamic_index_in_dim(table_t, c, 1, keepdims=False).reshape(16 * width, rows)
    other_table = lax.dynamic_index_in_dim(table_t, 1 - c, 1, keepdims=False).reshape(16 * width, rows)
    own_part = ring_place(across, across_near, across_far, y)
    own_part, own_table, other_table, both = tie((own_part, own_table, other_table, both))
    cols = lax.all_gather(both, "vocab", axis=0, axis_index_groups=same_core)

    pick_z = lambda d, part=own_part: lax.dynamic_index_in_dim(part, (z + d) % 4, 0, keepdims=False).reshape(4 * width, tokens)
    opposite = pick_z(2)
    hid_low, hid_high = send_z(pick_z(1), 1), send_z(pick_z(3), -1)
    mid = tokens // 2
    pass_low, pass_high = send_z(opposite[:, :mid], 1), send_z(opposite[:, mid:], -1)
    own_part = own_part.reshape(16 * width, tokens)
    other_part = send_core(own_part)
    logits = dot(own_table, own_part)
    logits, other_part = tie((logits, other_part))
    logits = logits + dot(other_table, other_part)
    pair_table = send_core(other_table)
    hot = target_ids[None, :] == entry
    top = jnp.max(logits, axis=0)
    total = jnp.sum(jnp.exp(logits - top[None, :]), axis=0)
    target = jnp.sum(jnp.where(hot, logits, 0.0), axis=0)
    stats = jnp.stack([top, total, target])
    stats = lax.all_to_all(jnp.broadcast_to(stats[None], (32,) + stats.shape), "vocab", 0, 0)
    stats, hid_low, hid_high = tie((stats, hid_low, hid_high))
    row_top = jnp.max(stats[:, 0], axis=0)
    exp_total = jnp.sum(stats[:, 1] * jnp.exp(stats[:, 0] - row_top[None]), axis=0)
    target_logit = jnp.sum(stats[:, 2], axis=0)
    log_norm = row_top + jnp.log(exp_total)
    token_loss = log_norm - target_logit

    grad = loss_scale[None, :] * (jnp.exp(logits - log_norm[None, :]) - hot.astype(F32))
    grad = grad.astype(BF)
    grad_low, grad_high = send_z(grad, 1), send_z(grad, -1)
    pair_grad = send_core(grad)
    terms, again = hidden_terms(own_table, pair_table, grad, pair_grad)
    terms = lax.all_to_all(terms.reshape(16, width, tokens), "vocab", 0, 0, axis_index_groups=same_core)
    cols, again, grad_low, grad_high, pass_low, pass_high = tie((cols, again, grad_low, grad_high, pass_low, pass_high))
    half = rows // 2
    hid_far = [send_z(pass_low, 1), send_z(pass_high, -1)]
    grad_far = [send_z(grad_low[:half], 1), send_z(grad_high[half:], -1)]
    cols = cols.reshape(4, 4, PAD, tokens)
    cots, hids, ids = [], [], []
    for block in order:
        piece = lax.dynamic_index_in_dim(cols, block, 0, keepdims=False)
        pair = piece[0, width : width + 2].astype(F32)
        ids.append((pair[0] * 256.0 + pair[1]).astype(jnp.int32))
        piece = piece[:, :width].reshape(4 * width, tokens)
        cots += [piece, send_core(piece)]
    for piece in (pick_z(0), hid_low, hid_high):
        hids += [piece, send_core(piece)]
    near = near_terms(cots, hids, jnp.stack(ids)[:, None], entry, [again, grad_low, grad_high])
    near, hid_far, grad_far = tie((near, hid_far, grad_far))
    hid_far = jnp.concatenate(hid_far, 1)
    grad_table = far_terms(
        c.astype(jnp.int32)[None], near, hid_far, send_core(hid_far), jnp.concatenate(grad_far, 0), width
    )
    terms, grad_table = tie((terms, grad_table))
    grad_hidden = jnp.sum(terms.astype(F32), axis=0).astype(BF).T
    return (grad_hidden, grad_table.reshape(8 * width, rows).T, token_loss)


def solution(mesh):
    placed = (P("seq", "vocab"), P("seq", "vocab"), P("vocab", None), P("seq"), P("seq"), P("seq"))
    return jax.shard_map(
        body,
        mesh=mesh,
        in_specs=placed,
        out_specs=(P("seq", "vocab"), P("vocab", "seq"), P("seq")),
        check_vma=False,
    )
```

```python
import jax
import jax.numpy as jnp
from jax import lax
from jax.experimental import pallas as pl
from jax.experimental.pallas import tpu as pltpu
from jax.sharding import PartitionSpec as P

BF, F32 = jnp.bfloat16, jnp.float32


def vocab_perm(move):
    pairs = []
    for v in range(32):
        y, x, c = move(v // 8, (v // 2) % 4, v % 2)
        pairs.append((v, (y % 4) * 8 + (x % 4) * 2 + c))
    return pairs


def send_x(a, d):
    return lax.ppermute(a, "vocab", vocab_perm(lambda y, x, c: (y, x + d, c)))


def send_y(a, d):
    return lax.ppermute(a, "vocab", vocab_perm(lambda y, x, c: (y + d, x, c)))


def send_core(a):
    return lax.ppermute(a, "vocab", vocab_perm(lambda y, x, c: (y, x, 1 - c)))


def send_z(a, d):
    return lax.ppermute(a, "seq", [(i, (i + d) % 4) for i in range(4)])


def swap_zy(a):
    pairs = []
    for z in range(4):
        for v in range(32):
            pairs.append((z * 32 + v, (v // 8) * 32 + z * 8 + v % 8))
    return lax.ppermute(a, ("seq", "vocab"), pairs)


def ring_near(a, send):
    return send(a, 1), send(a, -1)


def ring_far(near, send):
    low, high = near
    if low.ndim == 3:
        half = low.shape[0] // 2
        return send(low[:half], 1), send(high[half:], -1)
    half = low.shape[-1] // 2
    return send(low[..., :half], 1), send(high[..., half:], -1)


def ring_place(a, near, far, me):
    out = jnp.zeros((4,) + a.shape, a.dtype)
    out = lax.dynamic_update_index_in_dim(out, a, me, 0)
    out = lax.dynamic_update_index_in_dim(out, near[0], (me + 3) % 4, 0)
    out = lax.dynamic_update_index_in_dim(out, near[1], (me + 1) % 4, 0)
    return lax.dynamic_update_index_in_dim(out, jnp.concatenate(far, 0 if a.ndim == 3 else -1), (me + 2) % 4, 0)


PAD = 176
NN = (((1,), (0,)), ((), ()))


def mm(a, b):
    return lax.dot_general(a, b, NN, preferred_element_type=F32)


def hidden_kernel(own_ref, pair_ref, g_ref, pg_ref, out_ref, again_ref):
    again_ref[...] = g_ref[...]
    out_ref[...] = (mm(own_ref[...], g_ref[...]) + mm(pair_ref[...], pg_ref[...])).astype(BF)


def hidden_terms(own_table, pair_table, grad, pair_grad):
    rows, tokens = grad.shape
    columns, tile = own_table.shape[0], 672
    table = pl.BlockSpec((tile, rows), lambda i: (i, 0))
    whole = pl.BlockSpec((rows, tokens), lambda i: (0, 0))
    return pl.pallas_call(
        hidden_kernel,
        out_shape=[jax.ShapeDtypeStruct((columns, tokens), BF), jax.ShapeDtypeStruct((rows, tokens), BF)],
        grid=(columns // tile,),
        in_specs=[table, table, whole, whole],
        out_specs=[pl.BlockSpec((tile, tokens), lambda i: (i, 0)), whole],
        compiler_params=pltpu.CompilerParams(vmem_limit_bytes=56 << 20),
        cost_estimate=pl.CostEstimate(flops=4 << 30, bytes_accessed=12 << 20, transcendentals=0),
        name="hidden_terms",
    )(own_table, pair_table, grad, pair_grad)


NT = (((1,), (1,)), ((), ()))


def near_kernel(*refs):
    cots, hids, grads = refs[:8], refs[8:14], refs[16:19]
    ids_ref, entry_ref, acc_ref = refs[14], refs[15], refs[19]
    hots = [(ids_ref[k] == entry_ref[...]).astype(F32).astype(BF) for k in range(4)]
    for core in range(2):
        total = lax.dot_general(cots[core][...], hots[0], NT, preferred_element_type=F32)
        for k in range(1, 4):
            total += lax.dot_general(cots[2 * k + core][...], hots[k], NT, preferred_element_type=F32)
        for k in range(3):
            total += lax.dot_general(hids[2 * k + core][...], grads[k][...], NT, preferred_element_type=F32)
        acc_ref[core] = total


def near_terms(cots, hids, ids, entry, grads):
    rows, tokens = grads[0].shape
    columns, tile = cots[0].shape[0], 256
    return pl.pallas_call(
        near_kernel,
        out_shape=jax.ShapeDtypeStruct((2, columns, rows), F32),
        grid=(rows // tile,),
        in_specs=[pl.BlockSpec((columns, tokens), lambda i: (0, 0))] * 14
        + [pl.BlockSpec((4, 1, tokens), lambda i: (0, 0, 0)), pl.BlockSpec((tile, 1), lambda i: (i, 0))]
        + [pl.BlockSpec((tile, tokens), lambda i: (i, 0))] * 3,
        out_specs=pl.BlockSpec((2, columns, tile), lambda i: (0, 0, i)),
        compiler_params=pltpu.CompilerParams(vmem_limit_bytes=48 << 20),
        cost_estimate=pl.CostEstimate(flops=1 << 30, bytes_accessed=1 << 20, transcendentals=0),
        name="near_terms",
    )(*cots, *hids, ids, entry, *grads)


def far_kernel(core_ref, acc_ref, own_ref, other_ref, g_ref, out_ref):
    width, tile = out_ref.shape[2:]
    for core, ref in enumerate((own_ref, other_ref)):
        total = acc_ref[core] + lax.dot_general(ref[...], g_ref[...], NT, preferred_element_type=F32)
        place = core_ref[0] if core == 0 else 1 - core_ref[0]
        out_ref[:, pl.ds(place, 1)] = total.reshape(4, 1, width, tile)


def far_terms(core, acc, own, other, grad, width):
    rows, tokens = grad.shape
    columns, tile = own.shape[0], 256
    piece = pl.BlockSpec((columns, tokens), lambda i, core: (0, 0))
    return pl.pallas_call(
        far_kernel,
        out_shape=jax.ShapeDtypeStruct((4, 2, width, rows), F32),
        grid_spec=pltpu.PrefetchScalarGridSpec(
            num_scalar_prefetch=1,
            grid=(rows // tile,),
            in_specs=[
                pl.BlockSpec((2, columns, tile), lambda i, core: (0, 0, i)),
                piece,
                piece,
                pl.BlockSpec((tile, tokens), lambda i, core: (i, 0)),
            ],
            out_specs=pl.BlockSpec((4, 2, width, tile), lambda i, core: (0, 0, 0, i)),
        ),
        compiler_params=pltpu.CompilerParams(vmem_limit_bytes=32 << 20),
        cost_estimate=pl.CostEstimate(flops=1 << 30, bytes_accessed=8 << 20, transcendentals=0),
        name="far_terms",
    )(core, acc, own, other, grad)


def body(hidden, embed_cotangent, table, token_ids, target_ids, loss_scale):
    tie = lax.optimization_barrier
    z, v = lax.axis_index("seq"), lax.axis_index("vocab")
    y, x, c = v // 8, (v // 2) % 4, v % 2
    rows = table.shape[0]
    entry = v * rows + lax.broadcasted_iota(jnp.int32, (rows, 1), 0)
    order = [z, (z + 3) % 4, (z + 1) % 4, (z + 2) % 4]
    hid, cot = hidden.T, embed_cotangent.T
    width, tokens = hid.shape
    same_core = [[2 * k + i for k in range(16)] for i in range(2)]
    first = (((0,), (0,)), ((), ()))
    dot = lambda a, b: lax.dot_general(a, b, first, preferred_element_type=F32)

    id_rows = jnp.stack([token_ids // 256, token_ids % 256]).astype(BF)
    gap = PAD - width
    both = jnp.concatenate([cot, id_rows, jnp.zeros((gap - 2, tokens), BF)], 0)
    both = swap_zy(both)
    hid_near = ring_near(hid, send_x)
    hid_far = ring_far(hid_near, send_x)
    across = ring_place(hid, hid_near, hid_far, x)
    across, both = tie((across, both))
    across_near = ring_near(across, send_y)
    table_t = table.T.reshape(16, 2, width, rows)
    across_near, table_t = tie((across_near, table_t))
    across_far = ring_far(across_near, send_y)
    own_table = lax.dynamic_index_in_dim(table_t, c, 1, keepdims=False).reshape(16 * width, rows)
    other_table = lax.dynamic_index_in_dim(table_t, 1 - c, 1, keepdims=False).reshape(16 * width, rows)
    own_part = ring_place(across, across_near, across_far, y)
    own_part, own_table, other_table, both = tie((own_part, own_table, other_table, both))
    cols = lax.all_gather(both, "vocab", axis=0, axis_index_groups=same_core)

    pick_z = lambda d, part=own_part: lax.dynamic_index_in_dim(part, (z + d) % 4, 0, keepdims=False).reshape(4 * width, tokens)
    opposite = pick_z(2)
    hid_low, hid_high = send_z(pick_z(1), 1), send_z(pick_z(3), -1)
    mid = tokens // 2
    pass_low, pass_high = send_z(opposite[:, :mid], 1), send_z(opposite[:, mid:], -1)
    own_part = own_part.reshape(16 * width, tokens)
    other_part = send_core(own_part)
    logits = dot(own_table, own_part)
    logits, other_part = tie((logits, other_part))
    logits = logits + dot(other_table, other_part)
    pair_table = send_core(other_table)
    hot = target_ids[None, :] == entry
    top = jnp.max(logits, axis=0)
    total = jnp.sum(jnp.exp(logits - top[None, :]), axis=0)
    target = jnp.sum(jnp.where(hot, logits, 0.0), axis=0)
    stats = jnp.stack([top, total, target])
    stats = lax.all_to_all(jnp.broadcast_to(stats[None], (32,) + stats.shape), "vocab", 0, 0)
    stats, hid_low, hid_high, pass_low, pass_high = tie((stats, hid_low, hid_high, pass_low, pass_high))
    hid_far = [send_z(pass_low, 1), send_z(pass_high, -1)]
    row_top = jnp.max(stats[:, 0], axis=0)
    exp_total = jnp.sum(stats[:, 1] * jnp.exp(stats[:, 0] - row_top[None]), axis=0)
    target_logit = jnp.sum(stats[:, 2], axis=0)
    log_norm = row_top + jnp.log(exp_total)
    token_loss = log_norm - target_logit

    grad = loss_scale[None, :] * (jnp.exp(logits - log_norm[None, :]) - hot.astype(F32))
    grad = grad.astype(BF)
    grad_low, grad_high = send_z(grad, 1), send_z(grad, -1)
    pair_grad = send_core(grad)
    terms, again = hidden_terms(own_table, pair_table, grad, pair_grad)
    terms = lax.all_to_all(terms.reshape(16, width, tokens), "vocab", 0, 0, axis_index_groups=same_core)
    cols, again, grad_low, grad_high = tie((cols, again, grad_low, grad_high))
    half = rows // 2
    grad_far = [send_z(grad_low[:half], 1), send_z(grad_high[half:], -1)]
    cols = cols.reshape(4, 4, PAD, tokens)
    cots, hids, ids = [], [], []
    for block in order:
        piece = lax.dynamic_index_in_dim(cols, block, 0, keepdims=False)
        pair = piece[0, width : width + 2].astype(F32)
        ids.append((pair[0] * 256.0 + pair[1]).astype(jnp.int32))
        piece = piece[:, :width].reshape(4 * width, tokens)
        cots += [piece, send_core(piece)]
    for piece in (pick_z(0), hid_low, hid_high):
        hids += [piece, send_core(piece)]
    near = near_terms(cots, hids, jnp.stack(ids)[:, None], entry, [again, grad_low, grad_high])
    near, hid_far, grad_far = tie((near, hid_far, grad_far))
    hid_far = jnp.concatenate(hid_far, 1)
    grad_table = far_terms(
        c.astype(jnp.int32)[None], near, hid_far, send_core(hid_far), jnp.concatenate(grad_far, 0), width
    )
    terms, grad_table = tie((terms, grad_table))
    grad_hidden = jnp.sum(terms.astype(F32), axis=0).astype(BF).T
    return (grad_hidden, grad_table.reshape(8 * width, rows).T, token_loss)


def solution(mesh):
    placed = (P("seq", "vocab"), P("seq", "vocab"), P("vocab", None), P("seq"), P("seq"), P("seq"))
    return jax.shard_map(
        body,
        mesh=mesh,
        in_specs=placed,
        out_specs=(P("seq", "vocab"), P("vocab", "seq"), P("seq")),
        check_vma=False,
    )
```

```python
import jax
import jax.numpy as jnp
from jax import lax
from jax.experimental import pallas as pl
from jax.experimental.pallas import tpu as pltpu
from jax.sharding import PartitionSpec as P

BF, F32 = jnp.bfloat16, jnp.float32


def vocab_perm(move):
    pairs = []
    for v in range(32):
        y, x, c = move(v // 8, (v // 2) % 4, v % 2)
        pairs.append((v, (y % 4) * 8 + (x % 4) * 2 + c))
    return pairs


def send_x(a, d):
    return lax.ppermute(a, "vocab", vocab_perm(lambda y, x, c: (y, x + d, c)))


def send_y(a, d):
    return lax.ppermute(a, "vocab", vocab_perm(lambda y, x, c: (y + d, x, c)))


def send_core(a):
    return lax.ppermute(a, "vocab", vocab_perm(lambda y, x, c: (y, x, 1 - c)))


def send_z(a, d):
    return lax.ppermute(a, "seq", [(i, (i + d) % 4) for i in range(4)])


def swap_zy(a):
    pairs = []
    for z in range(4):
        for v in range(32):
            pairs.append((z * 32 + v, (v // 8) * 32 + z * 8 + v % 8))
    return lax.ppermute(a, ("seq", "vocab"), pairs)


def ring_near(a, send):
    return send(a, 1), send(a, -1)


def ring_far(near, send):
    low, high = near
    if low.ndim == 3:
        half = low.shape[0] // 2
        return send(low[:half], 1), send(high[half:], -1)
    half = low.shape[-1] // 2
    return send(low[..., :half], 1), send(high[..., half:], -1)


def ring_place(a, near, far, me):
    out = jnp.zeros((4,) + a.shape, a.dtype)
    out = lax.dynamic_update_index_in_dim(out, a, me, 0)
    out = lax.dynamic_update_index_in_dim(out, near[0], (me + 3) % 4, 0)
    out = lax.dynamic_update_index_in_dim(out, near[1], (me + 1) % 4, 0)
    return lax.dynamic_update_index_in_dim(out, jnp.concatenate(far, 0 if a.ndim == 3 else -1), (me + 2) % 4, 0)


PAD = 176
NN = (((1,), (0,)), ((), ()))


def mm(a, b):
    return lax.dot_general(a, b, NN, preferred_element_type=F32)


def hidden_kernel(own_ref, pair_ref, g_ref, pg_ref, out_ref, again_ref):
    again_ref[...] = g_ref[...]
    out_ref[...] = (mm(own_ref[...], g_ref[...]) + mm(pair_ref[...], pg_ref[...])).astype(BF)


def hidden_terms(own_table, pair_table, grad, pair_grad):
    rows, tokens = grad.shape
    columns, tile = own_table.shape[0], 672
    table = pl.BlockSpec((tile, rows), lambda i: (i, 0))
    whole = pl.BlockSpec((rows, tokens), lambda i: (0, 0))
    return pl.pallas_call(
        hidden_kernel,
        out_shape=[jax.ShapeDtypeStruct((columns, tokens), BF), jax.ShapeDtypeStruct((rows, tokens), BF)],
        grid=(columns // tile,),
        in_specs=[table, table, whole, whole],
        out_specs=[pl.BlockSpec((tile, tokens), lambda i: (i, 0)), whole],
        compiler_params=pltpu.CompilerParams(vmem_limit_bytes=56 << 20),
        cost_estimate=pl.CostEstimate(flops=4 << 30, bytes_accessed=12 << 20, transcendentals=0),
        name="hidden_terms",
    )(own_table, pair_table, grad, pair_grad)


NT = (((1,), (1,)), ((), ()))


def near_kernel(*refs):
    cots, hids, grads = refs[:8], refs[8:14], refs[16:19]
    ids_ref, entry_ref, acc_ref = refs[14], refs[15], refs[19]
    hots = [(ids_ref[k] == entry_ref[...]).astype(F32).astype(BF) for k in range(4)]
    for core in range(2):
        total = lax.dot_general(cots[core][...], hots[0], NT, preferred_element_type=F32)
        for k in range(1, 4):
            total += lax.dot_general(cots[2 * k + core][...], hots[k], NT, preferred_element_type=F32)
        for k in range(3):
            total += lax.dot_general(hids[2 * k + core][...], grads[k][...], NT, preferred_element_type=F32)
        acc_ref[core] = total


def near_terms(cots, hids, ids, entry, grads):
    rows, tokens = grads[0].shape
    columns, tile = cots[0].shape[0], 256
    return pl.pallas_call(
        near_kernel,
        out_shape=jax.ShapeDtypeStruct((2, columns, rows), F32),
        grid=(rows // tile,),
        in_specs=[pl.BlockSpec((columns, tokens), lambda i: (0, 0))] * 14
        + [pl.BlockSpec((4, 1, tokens), lambda i: (0, 0, 0)), pl.BlockSpec((tile, 1), lambda i: (i, 0))]
        + [pl.BlockSpec((tile, tokens), lambda i: (i, 0))] * 3,
        out_specs=pl.BlockSpec((2, columns, tile), lambda i: (0, 0, i)),
        compiler_params=pltpu.CompilerParams(vmem_limit_bytes=48 << 20),
        cost_estimate=pl.CostEstimate(flops=1 << 30, bytes_accessed=1 << 20, transcendentals=0),
        name="near_terms",
    )(*cots, *hids, ids, entry, *grads)


def far_kernel(core_ref, acc_ref, own_ref, other_ref, g_ref, out_ref):
    width, tile = out_ref.shape[2:]
    for core, ref in enumerate((own_ref, other_ref)):
        total = acc_ref[core] + lax.dot_general(ref[...], g_ref[...], NT, preferred_element_type=F32)
        place = core_ref[0] if core == 0 else 1 - core_ref[0]
        out_ref[:, pl.ds(place, 1)] = total.reshape(4, 1, width, tile)


def far_terms(core, acc, own, other, grad, width):
    rows, tokens = grad.shape
    columns, tile = own.shape[0], 256
    piece = pl.BlockSpec((columns, tokens), lambda i, core: (0, 0))
    return pl.pallas_call(
        far_kernel,
        out_shape=jax.ShapeDtypeStruct((4, 2, width, rows), F32),
        grid_spec=pltpu.PrefetchScalarGridSpec(
            num_scalar_prefetch=1,
            grid=(rows // tile,),
            in_specs=[
                pl.BlockSpec((2, columns, tile), lambda i, core: (0, 0, i)),
                piece,
                piece,
                pl.BlockSpec((tile, tokens), lambda i, core: (i, 0)),
            ],
            out_specs=pl.BlockSpec((4, 2, width, tile), lambda i, core: (0, 0, 0, i)),
        ),
        compiler_params=pltpu.CompilerParams(vmem_limit_bytes=32 << 20),
        cost_estimate=pl.CostEstimate(flops=1 << 30, bytes_accessed=8 << 20, transcendentals=0),
        name="far_terms",
    )(core, acc, own, other, grad)


def body(hidden, embed_cotangent, table, token_ids, target_ids, loss_scale):
    tie = lax.optimization_barrier
    z, v = lax.axis_index("seq"), lax.axis_index("vocab")
    y, x, c = v // 8, (v // 2) % 4, v % 2
    rows = table.shape[0]
    entry = v * rows + lax.broadcasted_iota(jnp.int32, (rows, 1), 0)
    order = [z, (z + 3) % 4, (z + 1) % 4, (z + 2) % 4]
    hid, cot = hidden.T, embed_cotangent.T
    width, tokens = hid.shape
    same_core = [[2 * k + i for k in range(16)] for i in range(2)]
    first = (((0,), (0,)), ((), ()))
    dot = lambda a, b: lax.dot_general(a, b, first, preferred_element_type=F32)

    id_rows = jnp.stack([token_ids // 256, token_ids % 256]).astype(BF)
    gap = PAD - width
    both = jnp.concatenate([cot, id_rows, jnp.zeros((gap - 2, tokens), BF)], 0)
    both = swap_zy(both)
    hid_near = ring_near(hid, send_x)
    hid_far = ring_far(hid_near, send_x)
    across = ring_place(hid, hid_near, hid_far, x)
    across, both = tie((across, both))
    across_near = ring_near(across, send_y)
    table_t = table.T.reshape(16, 2, width, rows)
    across_near, table_t = tie((across_near, table_t))
    across_far = ring_far(across_near, send_y)
    own_table = lax.dynamic_index_in_dim(table_t, c, 1, keepdims=False).reshape(16 * width, rows)
    other_table = lax.dynamic_index_in_dim(table_t, 1 - c, 1, keepdims=False).reshape(16 * width, rows)
    own_part = ring_place(across, across_near, across_far, y)
    own_part, own_table, other_table, both = tie((own_part, own_table, other_table, both))
    cols = lax.all_gather(both, "vocab", axis=0, axis_index_groups=same_core)

    pick_z = lambda d, part=own_part: lax.dynamic_index_in_dim(part, (z + d) % 4, 0, keepdims=False).reshape(4 * width, tokens)
    opposite = pick_z(2)
    hid_low, hid_high = send_z(pick_z(1), 1), send_z(pick_z(3), -1)
    mid = tokens // 2
    pass_low, pass_high = send_z(opposite[:, :mid], 1), send_z(opposite[:, mid:], -1)
    own_part = own_part.reshape(16 * width, tokens)
    other_part = send_core(own_part)
    logits = dot(own_table, own_part)
    logits, other_part = tie((logits, other_part))
    logits = logits + dot(other_table, other_part)
    pair_table = send_core(other_table)
    hot = target_ids[None, :] == entry
    top = jnp.max(logits, axis=0)
    total = jnp.sum(jnp.exp(logits - top[None, :]), axis=0)
    target = jnp.sum(jnp.where(hot, logits, 0.0), axis=0)
    stats = jnp.stack([top, total, target])
    stats = lax.all_to_all(jnp.broadcast_to(stats[None], (32,) + stats.shape), "vocab", 0, 0)
    stats, hid_low, hid_high = tie((stats, hid_low, hid_high))
    row_top = jnp.max(stats[:, 0], axis=0)
    exp_total = jnp.sum(stats[:, 1] * jnp.exp(stats[:, 0] - row_top[None]), axis=0)
    target_logit = jnp.sum(stats[:, 2], axis=0)
    log_norm = row_top + jnp.log(exp_total)
    token_loss = log_norm - target_logit

    grad = loss_scale[None, :] * (jnp.exp(logits - log_norm[None, :]) - hot.astype(F32))
    grad = grad.astype(BF)
    grad_low, grad_high = send_z(grad, 1), send_z(grad, -1)
    pair_grad = send_core(grad)
    terms, again = hidden_terms(own_table, pair_table, grad, pair_grad)
    terms = lax.all_to_all(terms.reshape(16, width, tokens), "vocab", 0, 0, axis_index_groups=same_core)
    cols, again, grad_low, grad_high, pass_low, pass_high = tie((cols, again, grad_low, grad_high, pass_low, pass_high))
    half = rows // 2
    hid_far = [send_z(pass_low, 1), send_z(pass_high, -1)]
    grad_far = [send_z(grad_low[:half], 1), send_z(grad_high[half:], -1)]
    cols = cols.reshape(4, 4, PAD, tokens)
    cots, hids, ids = [], [], []
    for block in order:
        piece = lax.dynamic_index_in_dim(cols, block, 0, keepdims=False)
        pair = piece[0, width : width + 2].astype(F32)
        ids.append((pair[0] * 256.0 + pair[1]).astype(jnp.int32))
        piece = piece[:, :width].reshape(4 * width, tokens)
        cots += [piece, send_core(piece)]
    for piece in (pick_z(0), hid_low, hid_high):
        hids += [piece, send_core(piece)]
    near = near_terms(cots, hids, jnp.stack(ids)[:, None], entry, [again, grad_low, grad_high])
    near, hid_far, grad_far = tie((near, hid_far, grad_far))
    hid_far = jnp.concatenate(hid_far, 1)
    grad_table = far_terms(
        c.astype(jnp.int32)[None], near, hid_far, send_core(hid_far), jnp.concatenate(grad_far, 0), width
    )
    terms, grad_table = tie((terms, grad_table))
    grad_hidden = jnp.sum(terms.astype(F32), axis=0).astype(BF).T
    return (grad_hidden, grad_table.reshape(8 * width, rows).T, token_loss)


def solution(mesh):
    placed = (P("seq", "vocab"), P("seq", "vocab"), P("vocab", None), P("seq"), P("seq"), P("seq"))
    return jax.shard_map(
        body,
        mesh=mesh,
        in_specs=placed,
        out_specs=(P("seq", "vocab"), P("vocab", "seq"), P("seq")),
        check_vma=False,
    )
```
